256 devices in a mesh: dp: 8 (over z), seq: 32 (over y, x, core).
Axes of the slice: x: 4, y: 4, z: 8, core: 2. Of those that a mesh axis runs over, the one named last changes fastest.
Arguments:
- query: bfloat16 [8, 4096, 4096], P('dp', 'seq'), may hold values from -1.796875 to 1.796875
- key_in: bfloat16 [8, 4096, 4096], P('dp', 'seq'), may hold values from -1.796875 to 1.796875
- value_in: bfloat16 [8, 4096, 4096], P('dp', 'seq'), may hold values from -17 to 17
- cotangent: bfloat16 [8, 4096, 4096], P('dp', 'seq'), may hold values from -6 to 6
- gain: float32 [4096], replicated, may hold values from 0.1 to 1.9
Outputs:
- grad_query: bfloat16 [8, 4096, 4096], P('dp', 'seq')
- grad_key: bfloat16 [8, 4096, 4096], P('dp', 'seq')
- grad_value: bfloat16 [8, 4096, 4096], P('dp', 'seq')
- grad_gain: float32 [4096], replicated
The draws below stay inside these ranges and needn't reach their ends.
All inputs are finite; a program needn't handle non-finite values.
Results may differ from the reference program's by a relative error of at most 0.011.
Values sent between devices are 32-bit elements; how exact they have to be, the bound alone decides.
A program may use at most 320 MiB of HBM per device.

```python
import jax
import jax.numpy as jnp
from jax import lax

HEADS = 32
HD = 128
TOK_DEV = 128
F = 4096
GROUPS = 8
SEQLEN = 4096


def draw_value_in(key, part):
    key = jax.random.fold_in(key, 7)
    first, second = jax.random.split(key)
    base = jnp.clip(jax.random.normal(first, (GROUPS, SEQLEN, HEADS * HD), jnp.float32), -5.0, 5.0)
    spread = jnp.exp(jax.random.uniform(second, (HEADS * HD,), jnp.float32, 0.0, 2.3))
    return (base * spread / 3.0).astype(jnp.bfloat16)


def block_scale(rng, extent, shards, least, high):
    level = 1.0
    for axis_at, shards_of in shards:
        steps = jax.random.uniform(jax.random.fold_in(jax.random.fold_in(rng, 6), axis_at), (shards_of,), jnp.float32, least / len(shards), high / len(shards))
        level = level * jnp.repeat(jnp.exp(steps), extent[axis_at] // shards_of).reshape((-1,) + (1,) * (len(extent) - 1 - axis_at))
    return level


def scatter_about(own_key, shape, deviation, bound, cuts=(), dtype=jnp.bfloat16):
    level = block_scale(own_key, shape, cuts, -0.22, 0.18) if cuts else 1.0
    result = jax.random.normal(own_key, shape, jnp.float32) * deviation * level
    return jnp.minimum(jnp.maximum(result, -bound), bound).astype(dtype)


def setup_inputs(seed: int = 0) -> dict:
    keys = jax.random.split(jax.random.key(seed), 6)
    return {
        "query": scatter_about(keys[0], (GROUPS, SEQLEN, F), 0.3, 1.796875, ((0, 8), (1, 32))),
        "key_in": scatter_about(keys[1], (GROUPS, SEQLEN, F), 0.3, 1.796875, ((0, 8), (1, 32))),
        "value_in": draw_value_in(jax.random.fold_in(keys[5], 71), 0),
        "cotangent": scatter_about(keys[3], (GROUPS, SEQLEN, F), 1.0, 6.0, ((0, 8), (1, 32))),
        "gain": jnp.clip(1.0 + 0.18 * jax.random.normal(keys[4], (F,), jnp.float32), 0.1, 1.9),
    }


HIGH = lax.Precision.HIGHEST

def group_backward(pieces):
    query, key_in, value_in, cotangent, gain = pieces
    blocks = SEQLEN // TOK_DEV
    shape_four = (blocks, TOK_DEV, HEADS, HD)
    q_all = query.reshape(shape_four)
    k_all = key_in.reshape(shape_four)
    v_all = value_in.reshape(shape_four)
    positions = jnp.arange(TOK_DEV)
    causal = (positions[:, None] >= positions[None, :])[None]
    zeros = jnp.zeros((HEADS, HD, HD), jnp.float32)

    def forward(prefix, items):
        q_blk, k_blk, v_blk = items
        q_f = q_blk.astype(jnp.float32)
        k_f = k_blk.astype(jnp.float32)
        v_f = v_blk.astype(jnp.float32)
        scores = jnp.einsum('thd,shd->hts', q_f, k_f, precision=HIGH)
        masked = jnp.where(causal, scores, 0.0).astype(jnp.bfloat16)
        attn = jnp.einsum('hts,she->the', masked.astype(jnp.float32), v_f, precision=HIGH)
        attn = attn + jnp.einsum('thd,hde->the', q_f, prefix, precision=HIGH)
        state = jnp.einsum('thd,the->hde', k_f, v_f, precision=HIGH)
        return (prefix + state, (attn, prefix))
    unused, (attn, prefixes) = lax.scan(forward, zeros, (q_all, k_all, v_all))
    flat = attn.reshape(blocks, TOK_DEV, HEADS * HD)
    dy_f = cotangent.reshape(blocks, TOK_DEV, HEADS * HD).astype(jnp.float32)
    scale = lax.rsqrt(lax.optimization_barrier(jnp.mean(flat * flat, axis=-1, keepdims=True)) + 1e-06)
    normed = flat * scale
    gain_term = lax.optimization_barrier(jnp.sum(dy_f * normed, axis=(0, 1)))
    dnorm = dy_f * gain
    inner = lax.optimization_barrier(jnp.mean(dnorm * normed, axis=-1, keepdims=True))
    grad_attn = (scale * (dnorm - normed * inner)).astype(jnp.bfloat16).reshape(shape_four)

    def backward(suffix, items):
        q_blk, k_blk, v_blk, d_blk, prefix = items
        q_f = q_blk.astype(jnp.float32)
        k_f = k_blk.astype(jnp.float32)
        v_f = v_blk.astype(jnp.float32)
        d_f = d_blk.astype(jnp.float32)
        scores = jnp.einsum('thd,shd->hts', q_f, k_f, precision=HIGH)
        masked = jnp.where(causal, scores, 0.0).astype(jnp.bfloat16).astype(jnp.float32)
        dscore = jnp.einsum('the,she->hts', d_f, v_f, precision=HIGH)
        dmask = jnp.where(causal, dscore, 0.0).astype(jnp.bfloat16).astype(jnp.float32)
        gstate = jnp.einsum('thd,the->hde', q_f, d_f, precision=HIGH)
        grad_q = jnp.einsum('hts,shd->thd', dmask, k_f, precision=HIGH) + jnp.einsum('the,hde->thd', d_f, prefix, precision=HIGH)
        grad_k = jnp.einsum('hts,thd->shd', dmask, q_f, precision=HIGH) + jnp.einsum('she,hde->shd', v_f, suffix, precision=HIGH)
        grad_v = jnp.einsum('hts,the->she', masked, d_f, precision=HIGH) + jnp.einsum('shd,hde->she', k_f, suffix, precision=HIGH)
        outs = (grad_q.astype(jnp.bfloat16), grad_k.astype(jnp.bfloat16), grad_v.astype(jnp.bfloat16))
        return (suffix + gstate, outs)
    unused, (grad_q, grad_k, grad_v) = lax.scan(backward, zeros, (q_all, k_all, v_all, grad_attn, prefixes), reverse=True)
    width = HEADS * HD
    return (grad_q.reshape(SEQLEN, width), grad_k.reshape(SEQLEN, width), grad_v.reshape(SEQLEN, width), gain_term)

def reference(query, key_in, value_in, cotangent, gain):
    gains = jnp.broadcast_to(gain, (GROUPS, HEADS * HD))
    grad_query, grad_key, grad_value, terms = lax.map(group_backward, (query, key_in, value_in, cotangent, gains))
    total = lax.optimization_barrier(jnp.sum(terms, axis=0))
    grad_gain = total / jnp.sqrt(jnp.float32(GROUPS * SEQLEN))
    return (grad_query, grad_key, grad_value, grad_gain)
```

```python
import functools
import math

import jax
import jax.numpy as jnp
from jax import lax
from jax.experimental import pallas as pl
from jax.experimental.pallas import tpu as pltpu
from jax.sharding import PartitionSpec as P

HD = 128
TOK = 128
HEADS = 32
F = HEADS * HD
HALF = HEADS // 2
SIDE = 4
CHIPS = SIDE * SIDE
DP = 8
G = 2
HG = HALF // G
MESH = pl.DeviceIdType.MESH
F32 = jnp.float32
BF16 = jnp.bfloat16

OFFSETS = [(dy, dx) for dy in range(SIDE) for dx in range(SIDE) if (dy, dx) != (0, 0)]
N_OFF = len(OFFSETS)


def dot(a, b, ca, cb):
    return lax.dot_general(a, b, (((ca,), (cb,)), ((), ())), preferred_element_type=F32)


def tiles(g, scan):
    return HG + (1 if scan == 1 and g == G - 1 else 0)


def scratch_shapes():
    shapes = {}
    for name in ("q", "k", "v", "dy"):
        shapes[name] = pltpu.VMEM((TOK, F), BF16)
    shapes["gain"] = pltpu.VMEM((1, F), F32)
    shapes["load_sem"] = pltpu.SemaphoreType.DMA((5,))
    for s in range(2):
        for g in range(G):
            n = tiles(g, s)
            shapes[f"own{s}{g}"] = pltpu.VMEM((2, CHIPS, n, 8, HD), F32)
            for name in ("pair", "sums", "gath", "give", "back", "hand", "taken"):
                shapes[f"{name}{s}{g}"] = pltpu.VMEM((CHIPS, n, 8, HD), F32)
        for name in ("out_s", "out_r", "back_s", "back_r"):
            shapes[f"{name}{s}"] = pltpu.SemaphoreType.DMA((G, N_OFF))
        for name in ("pair_s", "pair_r", "hand_s", "hand_r"):
            shapes[f"{name}{s}"] = pltpu.SemaphoreType.DMA((G,))
    shapes["prefix"] = pltpu.VMEM((HEADS, HD, HD), BF16)
    shapes["masked"] = pltpu.VMEM((HEADS, TOK, TOK), BF16)
    shapes["qt"] = pltpu.VMEM((HEADS, HD, TOK), BF16)
    shapes["attn"] = pltpu.VMEM((TOK, F), F32)
    shapes["dnorm"] = pltpu.VMEM((TOK, F), F32)
    shapes["grad"] = pltpu.VMEM((TOK, F), BF16)
    shapes["gk_part"] = pltpu.VMEM((TOK, F), F32)
    shapes["gv_part"] = pltpu.VMEM((TOK, F), F32)
    shapes["zrow"] = pltpu.VMEM((DP, 8, HD), F32)
    shapes["ztile"] = pltpu.VMEM((8, HD), F32)
    shapes["gtile"] = pltpu.VMEM((8, HD), F32)
    shapes["gback"] = pltpu.VMEM((CHIPS, 8, HD), F32)
    shapes["gtaken"] = pltpu.VMEM((CHIPS, 8, HD), F32)
    shapes["z_s"] = pltpu.SemaphoreType.DMA((DP - 1,))
    shapes["z_r"] = pltpu.SemaphoreType.DMA((DP - 1,))
    shapes["gb_s"] = pltpu.SemaphoreType.DMA((N_OFF,))
    shapes["gb_r"] = pltpu.SemaphoreType.DMA((N_OFF,))
    shapes["gp_s"] = pltpu.SemaphoreType.DMA((1,))
    shapes["gp_r"] = pltpu.SemaphoreType.DMA((1,))
    return shapes


NAMES = list(scratch_shapes())


def kernel(q_hbm, k_hbm, v_hbm, dy_hbm, gain_hbm, gq_ref, gk_ref, gv_ref, gg_ref, *scratch):
    m = dict(zip(NAMES, scratch))
    q, k, v, dy, gain = (m[n] for n in ("q", "k", "v", "dy", "gain"))
    loads = [
        pltpu.make_async_copy(src, dst, m["load_sem"].at[i])
        for i, (src, dst) in enumerate(((k_hbm, k), (v_hbm, v), (q_hbm, q), (dy_hbm, dy), (gain_hbm, gain)))
    ]
    for load in loads:
        load.start()

    z = lax.axis_index("dp")
    s_at = lax.axis_index("seq")
    chip = s_at // 2
    core = s_at % 2
    other = 1 - core
    y, x = chip // SIDE, chip % SIDE

    partner = (z, chip * 2 + other)
    near = [((y + dy_) % SIDE) * SIDE + (x + dx_) % SIDE for dy_, dx_ in OFFSETS]
    targets = [(z, c * 2 + core) for c in near]
    z_targets = [((z + d) % DP, s_at) for d in range(1, DP)]

    barrier = pltpu.get_barrier_semaphore()
    for t in [partner] + targets + z_targets:
        pl.semaphore_signal(barrier, inc=1, device_id=t, device_id_type=MESH)

    pending = []

    def remote(src, dst, ssem, rsem, target):
        copy = pltpu.make_async_remote_copy(
            src_ref=src, dst_ref=dst, send_sem=ssem, recv_sem=rsem, device_id=target, device_id_type=MESH
        )
        copy.start()
        pending.append(copy)
        return copy

    def lanes(head):
        return pl.ds(pl.multiple_of(head * HD, HD), HD)

    def each_head(first, count, step, body):
        def some(i, carry):
            for j in range(step):
                body(first + i * step + j, i * step + j)
            return carry

        lax.fori_loop(0, count // step, some, 0)

    def tile3(value):
        return value.reshape(CHIPS, 8, HD)

    def pair_send(scan, g):
        return remote(
            m[f"own{scan}{g}"].at[other], m[f"pair{scan}{g}"], m[f"pair_s{scan}"].at[g], m[f"pair_r{scan}"].at[g], partner
        )

    def out_send(scan, g):
        sums, gath = m[f"sums{scan}{g}"], m[f"gath{scan}{g}"]

        def add(c, carry):
            sums[c] = m[f"own{scan}{g}"][core, c] + m[f"pair{scan}{g}"][c]
            return carry

        lax.fori_loop(0, CHIPS, add, 0)
        gath[chip] = sums[chip]
        return [
            remote(sums.at[near[i]], gath.at[chip], m[f"out_s{scan}"].at[g, i], m[f"out_r{scan}"].at[g, i], targets[i])
            for i in range(N_OFF)
        ]

    def back_send(scan, g):
        gath, give, back = m[f"gath{scan}{g}"], m[f"give{scan}{g}"], m[f"back{scan}{g}"]

        def one(t, carry):
            total = jnp.zeros((8, HD), F32)
            for c in range(CHIPS) if scan == 0 else reversed(range(CHIPS)):
                give[c, t] = total
                total = total + gath[c, t]
            return carry

        lax.fori_loop(0, HG, one, 0)
        back[chip, :HG] = give[chip, :HG]
        return [
            remote(
                give.at[near[i], pl.ds(0, HG)],
                back.at[chip, pl.ds(0, HG)],
                m[f"back_s{scan}"].at[g, i],
                m[f"back_r{scan}"].at[g, i],
                targets[i],
            )
            for i in range(N_OFF)
        ]

    def hand_send(scan, g):
        hand = m[f"hand{scan}{g}"]
        with_own = jnp.where(core == (0 if scan == 0 else 1), 1.0, 0.0).astype(F32)

        def add(c, carry):
            hand[c, :HG] = m[f"back{scan}{g}"][c, :HG] + m[f"own{scan}{g}"][core, c, :HG] * with_own
            return carry

        lax.fori_loop(0, CHIPS, add, 0)
        return remote(
            hand.at[:, pl.ds(0, HG)],
            m[f"taken{scan}{g}"].at[:, pl.ds(0, HG)],
            m[f"hand_s{scan}"].at[g],
            m[f"hand_r{scan}"].at[g],
            partner,
        )

    def carried(scan, g, j, mine):
        if mine:
            with_pair = jnp.where(core == (1 if scan == 0 else 0), 1.0, 0.0).astype(F32)
            value = m[f"back{scan}{g}"][:, j] + m[f"pair{scan}{g}"][:, j] * with_pair
        else:
            value = m[f"taken{scan}{g}"][:, j]
        return value.reshape(HD, HD).astype(BF16)

    def states(half, g):
        def body(head, j):
            at = lanes(head)
            m[f"own0{g}"][half, :, j] = tile3(dot(k[:, at], v[:, at], 0, 0))

        each_head(half * HALF + g * HG, HG, 4, body)

    loads[0].wait()
    loads[1].wait()
    states(other, 0)
    pl.semaphore_wait(barrier, 1 + N_OFF + DP - 1)
    pairs = [pair_send(0, 0)]
    for g in range(1, G):
        states(other, g)
        pairs.append(pair_send(0, g))
    outs = []
    for g in range(G):
        states(core, g)
        pairs[g].wait_recv()
        outs.append(out_send(0, g))
    for load in loads[2:]:
        load.wait()

    rows = lax.broadcasted_iota(jnp.int32, (TOK, TOK), 0)
    cols = lax.broadcasted_iota(jnp.int32, (TOK, TOK), 1)
    causal = rows >= cols

    def local_part(head, j):
        at = lanes(head)
        q_h = q[:, at]
        scores = jnp.where(causal, dot(q_h, k[:, at], 1, 1), 0.0).astype(BF16)
        m["masked"][head] = scores
        m["attn"][:, at] = dot(scores, v[:, at], 1, 0)
        m["dnorm"][:, at] = dy[:, at].astype(F32) * gain[:, at]
        m["qt"][head] = q_h.T

    backs = []
    for g in range(G):
        each_head(g * (HEADS // G), HEADS // G, 4, local_part)
        for copy in outs[g]:
            copy.wait_recv()
        backs.append(back_send(0, g))
    hands = []
    for g in range(G):
        for copy in backs[g]:
            copy.wait_recv()
        hands.append(hand_send(0, g))

    sq = jnp.zeros((TOK, HD), F32)
    cross = jnp.zeros((TOK, HD), F32)

    def attn_part(half, g, mine, acc):
        def some(i, acc):
            sq, cross = acc
            for u in range(4):
                j = i * 4 + u
                head = half * HALF + g * HG + j
                at = lanes(head)
                p = carried(0, g, j, mine)
                m["prefix"][head] = p
                a = m["attn"][:, at] + dot(q[:, at], p, 1, 0)
                m["attn"][:, at] = a
                sq = sq + a * a
                cross = cross + a * m["dnorm"][:, at]
            return (sq, cross)

        return lax.fori_loop(0, HG // 4, some, acc)

    acc = (sq, cross)
    for g in range(G):
        acc = attn_part(core, g, True, acc)
    for g in range(G):
        hands[g].wait_recv()
        acc = attn_part(other, g, False, acc)
    sq, cross = acc
    scale = lax.rsqrt(jnp.sum(sq, axis=1, keepdims=True) * (1.0 / F) + 1e-06)
    inner = scale * (jnp.sum(cross, axis=1, keepdims=True) * (1.0 / F))
    scale = jnp.broadcast_to(scale, (TOK, HD))
    inner = jnp.broadcast_to(inner, (TOK, HD))

    def gstates(half, g):
        def body(head, j):
            at = lanes(head)
            normed = m["attn"][:, at] * scale
            grad = (scale * (m["dnorm"][:, at] - normed * inner)).astype(BF16)
            m["grad"][:, at] = grad
            term = tile3(dy[:, at].astype(F32) * normed).sum(axis=0)
            m[f"own1{G - 1}"][half, g * HG + j, HG] = term
            m[f"own1{g}"][half, :, j] = tile3(dot(m["qt"][head], grad, 1, 0))

        each_head(half * HALF + g * HG, HG, 4, body)

    pairs = []
    for g in range(G):
        gstates(other, g)
        pairs.append(pair_send(1, g))
    outs = []
    for g in range(G):
        gstates(core, g)
        pairs[g].wait_recv()
        outs.append(out_send(1, g))

    def grads_part(head, j):
        at = lanes(head)
        q_h, k_h, v_h, g_h = q[:, at], k[:, at], v[:, at], m["grad"][:, at]
        dmask = jnp.where(causal, dot(g_h, v_h, 1, 1), 0.0).astype(BF16)
        gq_ref[:, at] = (dot(dmask, k_h, 1, 0) + dot(g_h, m["prefix"][head], 1, 1)).astype(BF16)
        m["gk_part"][:, at] = dot(dmask, q_h, 0, 0)
        m["gv_part"][:, at] = dot(m["masked"][head], g_h, 0, 0)

    backs = []
    for g in range(G):
        each_head(g * (HEADS // G), HEADS // G, 4, grads_part)
        for copy in outs[g]:
            copy.wait_recv()
        if g == G - 1:
            gath = m[f"gath1{g}"]
            total = gath[0, HG]
            for c in range(1, CHIPS):
                total = total + gath[c, HG]
            m["ztile"][...] = total
            m["zrow"][z] = total
            zs = [
                remote(m["ztile"], m["zrow"].at[z], m["z_s"].at[i], m["z_r"].at[i], z_targets[i])
                for i in range(DP - 1)
            ]
        backs.append(back_send(1, g))

    for copy in zs:
        copy.wait_recv()
    total = m["zrow"][0]
    for i in range(1, DP):
        total = total + m["zrow"][i]
    total = jnp.sum(total, axis=0, keepdims=True) * (1.0 / math.sqrt(DP * 32 * TOK))
    total = jnp.broadcast_to(total, (8, HD))
    m["gtile"][...] = total
    m["gback"][chip] = total
    gbs = [
        remote(m["gtile"], m["gback"].at[chip], m["gb_s"].at[i], m["gb_r"].at[i], targets[i]) for i in range(N_OFF)
    ]

    hands = []
    for g in range(G):
        for copy in backs[g]:
            copy.wait_recv()
        hands.append(hand_send(1, g))

    def finish(half, g, mine):
        def body(head, j):
            at = lanes(head)
            s = carried(1, g, j, mine)
            gk_ref[:, at] = (m["gk_part"][:, at] + dot(v[:, at], s, 1, 1)).astype(BF16)
            gv_ref[:, at] = (m["gv_part"][:, at] + dot(k[:, at], s, 1, 0)).astype(BF16)

        each_head(half * HALF + g * HG, HG, 4, body)

    for g in range(G):
        finish(core, g, True)
    for copy in gbs:
        copy.wait_recv()
    gp = remote(m["gback"], m["gtaken"], m["gp_s"].at[0], m["gp_r"].at[0], partner)
    for g in range(G):
        hands[g].wait_recv()
        finish(other, g, False)
    gp.wait_recv()
    gg_ref[pl.ds(core * HALF, HALF)] = m["gback"][:, 0, :]
    gg_ref[pl.ds(other * HALF, HALF)] = m["gtaken"][:, 0, :]
    for copy in pending:
        copy.wait_send()


def shards(query, key_in, value_in, cotangent, gain):
    out = jax.ShapeDtypeStruct((TOK, F), BF16)
    vmem = pl.BlockSpec(memory_space=pltpu.VMEM)
    shapes = scratch_shapes()
    gq, gk, gv, gg = pl.pallas_call(
        kernel,
        out_shape=(out, out, out, jax.ShapeDtypeStruct((HEADS, HD), F32)),
        in_specs=[pl.BlockSpec(memory_space=pl.ANY)] * 5,
        out_specs=(vmem, vmem, vmem, vmem),
        scratch_shapes=[shapes[n] for n in NAMES],
        compiler_params=pltpu.CompilerParams(
            collective_id=0, has_side_effects=True, vmem_limit_bytes=60 * 2**20
        ),
        name="scan_grads",
    )(query[0], key_in[0], value_in[0], cotangent[0], gain.reshape(1, F))
    return gq[None], gk[None], gv[None], gg.reshape(F)


def solution(mesh):
    placed = P("dp", "seq", None)
    return jax.shard_map(
        shards,
        mesh=mesh,
        in_specs=(placed, placed, placed, placed, P()),
        out_specs=(placed, placed, placed, P()),
        check_vma=False,
    )
```

```python
import functools
import math

import jax
import jax.numpy as jnp
from jax import lax
from jax.experimental import pallas as pl
from jax.experimental.pallas import tpu as pltpu
from jax.sharding import PartitionSpec as P

HD = 128
TOK = 128
HEADS = 32
F = HEADS * HD
HALF = HEADS // 2
SIDE = 4
CHIPS = SIDE * SIDE
DP = 8
GROUPS = (8, 8)
G = len(GROUPS)
FIRST = [sum(GROUPS[:g]) for g in range(G)]
MESH = pl.DeviceIdType.MESH
F32 = jnp.float32
BF16 = jnp.bfloat16

OFFSETS = [(dy, dx) for dy in range(SIDE) for dx in range(SIDE) if (dy, dx) != (0, 0)]
N_OFF = len(OFFSETS)


def dot(a, b, ca, cb):
    return lax.dot_general(a, b, (((ca,), (cb,)), ((), ())), preferred_element_type=F32)


def tiles(g, scan):
    return GROUPS[g] + (1 if scan == 1 and g == G - 1 else 0)


def scratch_shapes():
    shapes = {}
    for name in ("q", "k", "v", "dy"):
        shapes[name] = pltpu.VMEM((TOK, F), BF16)
    shapes["gain"] = pltpu.VMEM((1, F), F32)
    shapes["load_sem"] = pltpu.SemaphoreType.DMA((5,))
    for s in range(2):
        for g in range(G):
            n = tiles(g, s)
            shapes[f"own{s}{g}"] = pltpu.VMEM((2, CHIPS, n, 8, HD), F32)
            for name in ("pair", "sums", "gath", "give", "back", "hand", "taken"):
                shapes[f"{name}{s}{g}"] = pltpu.VMEM((CHIPS, n, 8, HD), F32)
        for name in ("out_s", "out_r", "back_s", "back_r", "pair_s", "pair_r", "hand_s", "hand_r"):
            shapes[f"{name}{s}"] = pltpu.SemaphoreType.DMA((G,))
    shapes["prefix"] = pltpu.VMEM((HEADS, HD, HD), BF16)
    shapes["masked"] = pltpu.VMEM((HEADS, TOK, TOK), BF16)
    shapes["qt"] = pltpu.VMEM((HEADS, HD, TOK), BF16)
    shapes["attn"] = pltpu.VMEM((TOK, F), F32)
    shapes["dnorm"] = pltpu.VMEM((TOK, F), F32)
    shapes["grad"] = pltpu.VMEM((TOK, F), BF16)
    shapes["gk_part"] = pltpu.VMEM((TOK, F), F32)
    shapes["gv_part"] = pltpu.VMEM((TOK, F), F32)
    shapes["zrow"] = pltpu.VMEM((DP, 8, HD), F32)
    shapes["ztile"] = pltpu.VMEM((8, HD), F32)
    shapes["gtile"] = pltpu.VMEM((8, HD), F32)
    shapes["gback"] = pltpu.VMEM((CHIPS, 8, HD), F32)
    shapes["gtaken"] = pltpu.VMEM((CHIPS, 8, HD), F32)
    for name in ("z_s", "z_r", "gb_s", "gb_r", "gp_s", "gp_r"):
        shapes[name] = pltpu.SemaphoreType.DMA((1,))
    return shapes


NAMES = list(scratch_shapes())


def kernel(q_hbm, k_hbm, v_hbm, dy_hbm, gain_hbm, gq_ref, gk_ref, gv_ref, gg_ref, *scratch):
    m = dict(zip(NAMES, scratch))
    q, k, v, dy, gain = (m[n] for n in ("q", "k", "v", "dy", "gain"))
    loads = [
        pltpu.make_async_copy(src, dst, m["load_sem"].at[i])
        for i, (src, dst) in enumerate(((k_hbm, k), (v_hbm, v), (q_hbm, q), (dy_hbm, dy), (gain_hbm, gain)))
    ]
    for load in loads:
        load.start()

    z = lax.axis_index("dp")
    s_at = lax.axis_index("seq")
    chip = s_at // 2
    core = s_at % 2
    other = 1 - core
    y, x = chip // SIDE, chip % SIDE

    partner = (z, chip * 2 + other)
    near = [((y + dy_) % SIDE) * SIDE + (x + dx_) % SIDE for dy_, dx_ in OFFSETS]
    targets = [(z, c * 2 + core) for c in near]
    z_targets = [((z + d) % DP, s_at) for d in range(1, DP)]

    barrier = pltpu.get_barrier_semaphore()
    for t in [partner] + targets + z_targets:
        pl.semaphore_signal(barrier, inc=1, device_id=t, device_id_type=MESH)

    pending = []

    def wait_bytes(ref, sem):
        pltpu.make_async_copy(ref, ref, sem).wait()

    def remote(src, dst, ssem, rsem, target):
        copy = pltpu.make_async_remote_copy(
            src_ref=src, dst_ref=dst, send_sem=ssem, recv_sem=rsem, device_id=target, device_id_type=MESH
        )
        copy.start()
        return copy

    def fan(src_of, dst, ssem, rsem, to, whole):
        for i, target in enumerate(to):
            remote(src_of(i), dst, ssem, rsem, target)
        pending.append(lambda: wait_bytes(whole, ssem))
        return lambda: wait_bytes(whole, rsem)

    def to_partner(src, dst, ssem, rsem):
        copy = remote(src, dst, ssem, rsem, partner)
        pending.append(copy.wait_send)
        return copy.wait_recv

    def lanes(head):
        return pl.ds(pl.multiple_of(head * HD, HD), HD)

    def each_head(first, count, body, carry=0):
        step = 4 if count % 4 == 0 else 2

        def some(i, carry):
            for u in range(step):
                carry = body(first + i * step + u, i * step + u, carry)
            return carry

        return lax.fori_loop(0, count // step, some, carry)

    def tile3(value):
        return value.reshape(CHIPS, 8, HD)

    def pair_send(scan, g):
        return to_partner(
            m[f"own{scan}{g}"].at[other], m[f"pair{scan}{g}"], m[f"pair_s{scan}"].at[g], m[f"pair_r{scan}"].at[g]
        )

    def out_send(scan, g):
        sums, gath = m[f"sums{scan}{g}"], m[f"gath{scan}{g}"]

        def add(c, carry):
            sums[c] = m[f"own{scan}{g}"][core, c] + m[f"pair{scan}{g}"][c]
            return carry

        lax.fori_loop(0, CHIPS, add, 0)
        gath[chip] = sums[chip]
        return fan(
            lambda i: sums.at[near[i]],
            gath.at[chip],
            m[f"out_s{scan}"].at[g],
            m[f"out_r{scan}"].at[g],
            targets,
            gath.at[pl.ds(0, N_OFF)],
        )

    def back_send(scan, g):
        gath, give, back = m[f"gath{scan}{g}"], m[f"give{scan}{g}"], m[f"back{scan}{g}"]

        def one(t, carry):
            total = jnp.zeros((8, HD), F32)
            for c in range(CHIPS) if scan == 0 else reversed(range(CHIPS)):
                give[c, t] = total
                total = total + gath[c, t]
            return carry

        lax.fori_loop(0, GROUPS[g], one, 0)
        back[chip, :GROUPS[g]] = give[chip, :GROUPS[g]]
        heads = pl.ds(0, GROUPS[g])
        return fan(
            lambda i: give.at[near[i], heads],
            back.at[chip, heads],
            m[f"back_s{scan}"].at[g],
            m[f"back_r{scan}"].at[g],
            targets,
            back.at[pl.ds(0, N_OFF), heads],
        )

    def hand_send(scan, g):
        hand = m[f"hand{scan}{g}"]
        with_own = jnp.where(core == (0 if scan == 0 else 1), 1.0, 0.0).astype(F32)

        def add(c, carry):
            hand[c, :GROUPS[g]] = m[f"back{scan}{g}"][c, :GROUPS[g]] + m[f"own{scan}{g}"][core, c, :GROUPS[g]] * with_own
            return carry

        lax.fori_loop(0, CHIPS, add, 0)
        return to_partner(
            hand.at[:, pl.ds(0, GROUPS[g])],
            m[f"taken{scan}{g}"].at[:, pl.ds(0, GROUPS[g])],
            m[f"hand_s{scan}"].at[g],
            m[f"hand_r{scan}"].at[g],
        )

    def carried(scan, g, j, mine):
        if mine:
            with_pair = jnp.where(core == (1 if scan == 0 else 0), 1.0, 0.0).astype(F32)
            value = m[f"back{scan}{g}"][:, j] + m[f"pair{scan}{g}"][:, j] * with_pair
        else:
            value = m[f"taken{scan}{g}"][:, j]
        return value.reshape(HD, HD).astype(BF16)

    def states(half, g):
        def body(head, j, carry):
            at = lanes(head)
            m[f"own0{g}"][half, :, j] = tile3(dot(k[:, at], v[:, at], 0, 0))
            return carry

        each_head(half * HALF + FIRST[g], GROUPS[g], body)

    loads[0].wait()
    loads[1].wait()
    for g in range(G):
        states(other, g)
    states(core, 0)
    pl.semaphore_wait(barrier, 1 + N_OFF + DP - 1)
    pairs = [pair_send(0, g) for g in range(G)]
    for g in range(1, G):
        states(core, g)
    outs = []
    for g in range(G):
        pairs[g]()
        outs.append(out_send(0, g))
    for load in loads[2:]:
        load.wait()

    rows = lax.broadcasted_iota(jnp.int32, (TOK, TOK), 0)
    cols = lax.broadcasted_iota(jnp.int32, (TOK, TOK), 1)
    causal = rows >= cols

    def local_part(head, j, carry):
        at = lanes(head)
        scores = jnp.where(causal, dot(q[:, at], k[:, at], 1, 1), 0.0).astype(BF16)
        m["masked"][head] = scores
        m["attn"][:, at] = dot(scores, v[:, at], 1, 0)
        return carry

    def later_part(head, j, carry):
        at = lanes(head)
        m["dnorm"][:, at] = dy[:, at].astype(F32) * gain[:, at]
        m["qt"][head] = q[:, at].T
        return carry

    backs = []
    for g in range(G):
        each_head(2 * FIRST[g], 2 * GROUPS[g], local_part)
        outs[g]()
        backs.append(back_send(0, g))
    each_head(0, HEADS, later_part)

    def attn_part(half, g, mine, acc):
        def body(head, j, acc):
            sq, cross = acc
            at = lanes(head)
            p = carried(0, g, j, mine)
            m["prefix"][head] = p
            a = m["attn"][:, at] + dot(q[:, at], p, 1, 0)
            m["attn"][:, at] = a
            return (sq + a * a, cross + a * m["dnorm"][:, at])

        return each_head(half * HALF + FIRST[g], GROUPS[g], body, acc)

    acc = (jnp.zeros((TOK, HD), F32), jnp.zeros((TOK, HD), F32))
    for g in range(G):
        backs[g]()
        hand = hand_send(0, g)
        acc = attn_part(core, g, True, acc)
        hand()
        acc = attn_part(other, g, False, acc)
    sq, cross = acc
    scale = lax.rsqrt(jnp.sum(sq, axis=1, keepdims=True) * (1.0 / F) + 1e-06)
    inner = scale * (jnp.sum(cross, axis=1, keepdims=True) * (1.0 / F))
    scale = jnp.broadcast_to(scale, (TOK, HD))
    inner = jnp.broadcast_to(inner, (TOK, HD))

    def gstates(half, g):
        def body(head, j, carry):
            at = lanes(head)
            normed = m["attn"][:, at] * scale
            grad = (scale * (m["dnorm"][:, at] - normed * inner)).astype(BF16)
            m["grad"][:, at] = grad
            term = tile3(dy[:, at].astype(F32) * normed).sum(axis=0)
            m[f"own1{G - 1}"][half, FIRST[g] + j, GROUPS[G - 1]] = term
            m[f"own1{g}"][half, :, j] = tile3(dot(m["qt"][head], grad, 1, 0))
            return carry

        each_head(half * HALF + FIRST[g], GROUPS[g], body)

    pairs = []
    for g in range(G):
        gstates(other, g)
        pairs.append(pair_send(1, g))
    outs = []
    for g in range(G):
        gstates(core, g)
        pairs[g]()
        outs.append(out_send(1, g))

    def grads_part(head, j, carry):
        at = lanes(head)
        g_h = m["grad"][:, at]
        dmask = jnp.where(causal, dot(g_h, v[:, at], 1, 1), 0.0).astype(BF16)
        gq_ref[:, at] = (dot(dmask, k[:, at], 1, 0) + dot(g_h, m["prefix"][head], 1, 1)).astype(BF16)
        m["gk_part"][:, at] = dot(dmask, q[:, at], 0, 0)
        return carry

    def value_part(head, j, carry):
        at = lanes(head)
        m["gv_part"][:, at] = dot(m["masked"][head], m["grad"][:, at], 0, 0)
        return carry

    backs = []
    for g in range(G):
        each_head(2 * FIRST[g], 2 * GROUPS[g], grads_part)
        outs[g]()
        if g == G - 1:
            gath = m[f"gath1{g}"]
            total = gath[0, GROUPS[g]]
            for c in range(1, CHIPS):
                total = total + gath[c, GROUPS[g]]
            m["ztile"][...] = total
            m["zrow"][z] = total
            zs = fan(
                lambda i: m["ztile"], m["zrow"].at[z], m["z_s"].at[0], m["z_r"].at[0], z_targets, m["zrow"].at[pl.ds(0, DP - 1)]
            )
        backs.append(back_send(1, g))
    each_head(0, HEADS, value_part)

    def finish(half, g, mine):
        def body(head, j, carry):
            at = lanes(head)
            s = carried(1, g, j, mine)
            gk_ref[:, at] = (m["gk_part"][:, at] + dot(v[:, at], s, 1, 1)).astype(BF16)
            gv_ref[:, at] = (m["gv_part"][:, at] + dot(k[:, at], s, 1, 0)).astype(BF16)
            return carry

        each_head(half * HALF + FIRST[g], GROUPS[g], body)

    for g in range(G):
        if g == G - 1:
            zs()
            total = m["zrow"][0]
            for i in range(1, DP):
                total = total + m["zrow"][i]
            total = jnp.sum(total, axis=0, keepdims=True) * (1.0 / math.sqrt(DP * 32 * TOK))
            total = jnp.broadcast_to(total, (8, HD))
            m["gtile"][...] = total
            m["gback"][chip] = total
            gbs = fan(
                lambda i: m["gtile"], m["gback"].at[chip], m["gb_s"].at[0], m["gb_r"].at[0], targets, m["gback"].at[pl.ds(0, N_OFF)]
            )
        backs[g]()
        hand = hand_send(1, g)
        finish(core, g, True)
        if g == G - 1:
            gbs()
            gp = to_partner(m["gback"], m["gtaken"], m["gp_s"].at[0], m["gp_r"].at[0])
        hand()
        finish(other, g, False)
    gg_ref[pl.ds(core * HALF, HALF)] = m["gback"][:, 0, :]
    gp()
    gg_ref[pl.ds(other * HALF, HALF)] = m["gtaken"][:, 0, :]
    for wait in pending:
        wait()


def write_out(*refs):
    ins, outs, sem = refs[:4], refs[4:8], refs[8]
    copies = [pltpu.make_async_copy(i, o, sem.at[n]) for n, (i, o) in enumerate(zip(ins, outs))]
    for copy in copies:
        copy.start()
    for copy in copies:
        copy.wait()


def shards(query, key_in, value_in, cotangent, gain):
    shapes = scratch_shapes()
    vmem = pl.BlockSpec(memory_space=pltpu.VMEM)
    hbm = pl.BlockSpec(memory_space=pl.ANY)
    kept = (pltpu.VMEM((TOK, F), BF16),) * 3 + (pltpu.VMEM((HEADS, HD), F32),)
    results = pl.pallas_call(
        kernel,
        out_shape=kept,
        in_specs=[hbm] * 5,
        out_specs=(vmem,) * 4,
        scratch_shapes=[shapes[n] for n in NAMES],
        compiler_params=pltpu.CompilerParams(
            collective_id=0, has_side_effects=True, vmem_limit_bytes=60 * 2**20
        ),
        name="scan_grads",
    )(query[0], key_in[0], value_in[0], cotangent[0], gain.reshape(1, F))
    gq, gk, gv, gg = pl.pallas_call(
        write_out,
        out_shape=tuple(jax.ShapeDtypeStruct(r.shape, r.dtype) for r in results),
        in_specs=[vmem] * 4,
        out_specs=(hbm,) * 4,
        scratch_shapes=[pltpu.SemaphoreType.DMA((4,))],
        compiler_params=pltpu.CompilerParams(vmem_limit_bytes=8 * 2**20),
        name="write_out",
    )(*results)
    return gq[None], gk[None], gv[None], gg.reshape(F)


def solution(mesh):
    placed = P("dp", "seq", None)
    return jax.shard_map(
        shards,
        mesh=mesh,
        in_specs=(placed, placed, placed, placed, P()),
        out_specs=(placed, placed, placed, P()),
        check_vma=False,
    )
```

```python
import functools
import math

import jax
import jax.numpy as jnp
from jax import lax
from jax.experimental import pallas as pl
from jax.experimental.pallas import tpu as pltpu
from jax.sharding import PartitionSpec as P

HD = 128
TOK = 128
HEADS = 32
F = HEADS * HD
HALF = HEADS // 2
SIDE = 4
ROWS = HD // SIDE
DP = 8
GROUPS = (4, 4, 4, 4)
G = len(GROUPS)
FIRST = [sum(GROUPS[:g]) for g in range(G)]
LEAD = 2
GAIN_POINTS = ("F0", "F2", "F3", "E", "B2")
MESH = pl.DeviceIdType.MESH
F32 = jnp.float32
BF16 = jnp.bfloat16

def dot(a, b, ca, cb):
    return lax.dot_general(a, b, (((ca,), (cb,)), ((), ())), preferred_element_type=F32)


def scratch_shapes():
    shapes = {}
    for name in ("q", "k", "v", "dy"):
        shapes[name] = pltpu.VMEM((TOK, F), BF16)
    shapes["gain"] = pltpu.VMEM((1, F), F32)
    shapes["load_sem"] = pltpu.SemaphoreType.DMA((5,))
    for s in range(2):
        for g in range(G):
            n = GROUPS[g]
            shapes[f"own{s}{g}"] = pltpu.VMEM((2, SIDE, n, ROWS, HD), F32)
            shapes[f"total{s}{g}"] = pltpu.VMEM((n, ROWS, HD), F32)
            for name in ("pair", "sums", "gath", "rows", "give", "back", "hand", "taken"):
                shapes[f"{name}{s}{g}"] = pltpu.VMEM((SIDE, n, ROWS, HD), F32)
        for name in ("pair", "out", "rows", "back", "hand"):
            shapes[f"{name}_s{s}"] = pltpu.SemaphoreType.DMA((G,))
            shapes[f"{name}_r{s}"] = pltpu.SemaphoreType.DMA((G,))
    shapes["prefix"] = pltpu.VMEM((HEADS, HD, HD), BF16)
    shapes["masked"] = pltpu.VMEM((HEADS, TOK, TOK), BF16)
    shapes["qt"] = pltpu.VMEM((HEADS, HD, TOK), BF16)
    shapes["attn"] = pltpu.VMEM((TOK, F), F32)
    shapes["dnorm"] = pltpu.VMEM((TOK, F), F32)
    shapes["grad"] = pltpu.VMEM((TOK, F), BF16)
    shapes["gk_part"] = pltpu.VMEM((TOK, F), F32)
    shapes["gv_part"] = pltpu.VMEM((TOK, F), F32)
    shapes["gain_own"] = pltpu.VMEM((2, SIDE, ROWS, HD), F32)
    for name in ("gain_pair", "gain_sums", "gain_x", "gain_y", "gain_back", "gain_taken"):
        shapes[name] = pltpu.VMEM((SIDE, ROWS, HD), F32)
    shapes["gain_z"] = pltpu.VMEM((DP, ROWS, HD), F32)
    for name in ("gain_ysend", "gain_zsend", "gain_bsend"):
        shapes[name] = pltpu.VMEM((ROWS, HD), F32)
    shapes["gain_s"] = pltpu.SemaphoreType.DMA((6,))
    shapes["gain_r"] = pltpu.SemaphoreType.DMA((6,))
    return shapes


NAMES = list(scratch_shapes())


def kernel(q_hbm, k_hbm, v_hbm, dy_hbm, gain_hbm, gq_ref, gk_ref, gv_ref, gg_ref, *scratch):
    m = dict(zip(NAMES, scratch))
    q, k, v, dy, gain = (m[n] for n in ("q", "k", "v", "dy", "gain"))
    loads = [
        pltpu.make_async_copy(src, dst, m["load_sem"].at[i])
        for i, (src, dst) in enumerate(((k_hbm, k), (v_hbm, v), (q_hbm, q), (dy_hbm, dy), (gain_hbm, gain)))
    ]
    for load in loads:
        load.start()

    z = lax.axis_index("dp")
    s_at = lax.axis_index("seq")
    chip = s_at // 2
    core = s_at % 2
    other = 1 - core
    y, x = chip // SIDE, chip % SIDE

    def device(y_at, x_at, core_at):
        return (z, (y_at * SIDE + x_at) * 2 + core_at)

    partner = device(y, x, other)
    turns = [2, 1 + 2 * core, 3 - 2 * core]
    x_near = [(x + d) % SIDE for d in turns]
    x_targets = [device(y, c, core) for c in x_near]
    y_targets = [device((y + d) % SIDE, x, core) for d in turns]
    z_targets = [((z + d) % DP, s_at) for d in (1, 7, 2, 6, 3, 5, 4)]

    barrier = pltpu.get_barrier_semaphore()
    greeted = [partner] + x_targets + y_targets + z_targets
    for t in greeted:
        pl.semaphore_signal(barrier, inc=1, device_id=t, device_id_type=MESH)

    pending = []

    def wait_bytes(ref, sem):
        pltpu.make_async_copy(ref, ref, sem).wait()

    def remote(src, dst, ssem, rsem, target):
        copy = pltpu.make_async_remote_copy(
            src_ref=src, dst_ref=dst, send_sem=ssem, recv_sem=rsem, device_id=target, device_id_type=MESH
        )
        copy.start()
        return copy

    def fan(src_of, dst, ssem, rsem, to, whole):
        for i, target in enumerate(to):
            remote(src_of(i), dst, ssem, rsem, target)
        pending.append(lambda: wait_bytes(whole, ssem))
        return lambda: wait_bytes(whole, rsem)

    def to_partner(src, dst, ssem, rsem):
        copy = remote(src, dst, ssem, rsem, partner)
        pending.append(copy.wait_send)
        return copy.wait_recv

    def lanes(head):
        return pl.ds(pl.multiple_of(head * HD, HD), HD)

    def each_head(first, count, body, carry=0):
        step = 4 if count % 4 == 0 else 2

        def some(i, carry):
            for u in range(step):
                carry = body(first + i * step + u, i * step + u, carry)
            return carry

        return lax.fori_loop(0, count // step, some, carry)

    def sliced(value):
        return value.reshape(SIDE, ROWS, HD)

    def sems(name, scan, g):
        return m[f"{name}_s{scan}"].at[g], m[f"{name}_r{scan}"].at[g]

    def pair_send(scan, g):
        return to_partner(m[f"own{scan}{g}"].at[other], m[f"pair{scan}{g}"], *sems("pair", scan, g))

    def out_send(scan, g):
        sums, gath = m[f"sums{scan}{g}"], m[f"gath{scan}{g}"]

        def add(c, carry):
            sums[c] = m[f"own{scan}{g}"][core, c] + m[f"pair{scan}{g}"][c]
            return carry

        lax.fori_loop(0, SIDE, add, 0)
        gath[x] = sums[x]
        return fan(
            lambda i: sums.at[x_near[i]], gath.at[x], *sems("out", scan, g), x_targets, gath.at[pl.ds(0, SIDE - 1)]
        )

    def rows_send(scan, g):
        gath, total, rows = m[f"gath{scan}{g}"], m[f"total{scan}{g}"], m[f"rows{scan}{g}"]

        def one(j, carry):
            value = (gath[0, j] + gath[1, j]) + (gath[2, j] + gath[3, j])
            total[j] = value
            rows[y, j] = value
            return carry

        lax.fori_loop(0, GROUPS[g], one, 0)
        return fan(lambda i: total, rows.at[y], *sems("rows", scan, g), y_targets, rows.at[pl.ds(0, SIDE - 1)])

    def back_send(scan, g):
        gath, rows, give, back = (m[f"{name}{scan}{g}"] for name in ("gath", "rows", "give", "back"))

        def one(j, carry):
            value = jnp.zeros((ROWS, HD), F32)
            for c in range(SIDE):
                value = value + jnp.where(c < y if scan == 0 else c > y, rows[c, j], 0.0)
            for c in range(SIDE) if scan == 0 else reversed(range(SIDE)):
                give[c, j] = value
                value = value + gath[c, j]
            return carry

        lax.fori_loop(0, GROUPS[g], one, 0)
        back[x] = give[x]
        return fan(
            lambda i: give.at[x_near[i]],
            back.at[x],
            *sems("back", scan, g),
            x_targets,
            back.at[pl.ds(0, SIDE - 1)],
        )

    def hand_send(scan, g):
        hand, back, own = (m[f"{name}{scan}{g}"] for name in ("hand", "back", "own"))
        with_own = jnp.where(core == (0 if scan == 0 else 1), 1.0, 0.0).astype(F32)

        def add(c, carry):
            hand[c] = back[c] + own[core, c] * with_own
            return carry

        lax.fori_loop(0, SIDE, add, 0)
        return to_partner(hand, m[f"taken{scan}{g}"], *sems("hand", scan, g))

    def carried(scan, g, j, mine):
        if mine:
            with_pair = jnp.where(core == (1 if scan == 0 else 0), 1.0, 0.0).astype(F32)
            value = m[f"back{scan}{g}"][:, j] + m[f"pair{scan}{g}"][:, j] * with_pair
        else:
            value = m[f"taken{scan}{g}"][:, j]
        return value.reshape(HD, HD).astype(BF16)

    def exchange(scan, pairs, ready, fill):
        outs, totals, backs = [], [], []
        for g in range(LEAD):
            ready(g)
            pairs[g]()
            outs.append(out_send(scan, g))
        for g in range(G):
            fill(g)
            outs[g]()
            totals.append(rows_send(scan, g))
            if g + LEAD < G:
                pairs[g + LEAD]()
                outs.append(out_send(scan, g + LEAD))
            if g >= 1:
                totals[g - 1]()
                backs.append(back_send(scan, g - 1))
        totals[G - 1]()
        backs.append(back_send(scan, G - 1))
        return backs

    gain_wait = []

    def gain_step(at):
        step_sems = (m["gain_s"].at[at], m["gain_r"].at[at])
        if at:
            gain_wait[at - 1]()
        if at == 0:
            wait = to_partner(m["gain_own"].at[other], m["gain_pair"], *step_sems)
        elif at == 1:
            sums, got = m["gain_sums"], m["gain_x"]
            sums[...] = m["gain_own"][core] + m["gain_pair"][...]
            got[x] = sums[x]
            wait = fan(lambda i: sums.at[x_near[i]], got.at[x], *step_sems, x_targets, got.at[pl.ds(0, SIDE - 1)])
        elif at == 2:
            wait = gain_fan("gain_x", "gain_ysend", "gain_y", y, y_targets, step_sems)
        elif at == 3:
            wait = gain_fan("gain_y", "gain_zsend", "gain_z", z, z_targets, step_sems)
        elif at == 4:
            wait = gain_fan("gain_z", "gain_bsend", "gain_back", x, x_targets, step_sems)
        else:
            wait = to_partner(m["gain_back"], m["gain_taken"], *step_sems)
        gain_wait.append(wait)

    def gain_fan(src, send, dst, slot, to, step_sems):
        value = jnp.sum(m[src][...], axis=0)
        m[send][...] = value
        m[dst][slot] = value
        return fan(lambda i: m[send], m[dst].at[slot], *step_sems, to, m[dst].at[pl.ds(0, len(to))])

    def gain_result(ref):
        total = ref[...].reshape(HALF, 8, HD).sum(axis=1)
        return total * (1.0 / math.sqrt(DP * 32 * TOK))

    def states(half, g):
        def body(head, j, carry):
            at = lanes(head)
            m[f"own0{g}"][half, :, j] = sliced(dot(k[:, at], v[:, at], 0, 0))
            return carry

        each_head(half * HALF + FIRST[g], GROUPS[g], body)

    loads[0].wait()
    loads[1].wait()
    for g in range(G):
        states(other, g)
    states(core, 0)
    pl.semaphore_wait(barrier, len(greeted))
    pairs = [pair_send(0, g) for g in range(G)]
    for g in range(1, G):
        states(core, g)
    for load in loads[2:]:
        load.wait()

    rows = lax.broadcasted_iota(jnp.int32, (TOK, TOK), 0)
    cols = lax.broadcasted_iota(jnp.int32, (TOK, TOK), 1)
    causal = rows >= cols

    def local_part(head, j, carry):
        at = lanes(head)
        scores = jnp.where(causal, dot(q[:, at], k[:, at], 1, 1), 0.0).astype(BF16)
        m["masked"][head] = scores
        m["attn"][:, at] = dot(scores, v[:, at], 1, 0)
        return carry

    def later_part(head, j, carry):
        at = lanes(head)
        m["dnorm"][:, at] = dy[:, at].astype(F32) * gain[:, at]
        m["qt"][head] = q[:, at].T
        return carry

    def part(body, g):
        each_head(2 * FIRST[g], 2 * GROUPS[g], body)

    def fill(g):
        if g == 0:
            part(local_part, 0)
            part(local_part, 1)
        elif g < G - 1:
            part(local_part, g + 1)
        else:
            each_head(0, HEADS, later_part)

    backs = exchange(0, pairs, lambda g: None, fill)

    def attn_part(half, g, mine, acc):
        def body(head, j, acc):
            sq, cross = acc
            at = lanes(head)
            p = carried(0, g, j, mine)
            m["prefix"][head] = p
            a = m["attn"][:, at] + dot(q[:, at], p, 1, 0)
            m["attn"][:, at] = a
            return (sq + a * a, cross + a * m["dnorm"][:, at])

        return each_head(half * HALF + FIRST[g], GROUPS[g], body, acc)

    acc = (jnp.zeros((TOK, HD), F32), jnp.zeros((TOK, HD), F32))
    for g in range(G):
        backs[g]()
        hand = hand_send(0, g)
        acc = attn_part(core, g, True, acc)
        hand()
        acc = attn_part(other, g, False, acc)
    sq, cross = acc
    scale = lax.rsqrt(jnp.sum(sq, axis=1, keepdims=True) * (1.0 / F) + 1e-06)
    inner = scale * (jnp.sum(cross, axis=1, keepdims=True) * (1.0 / F))
    scale = jnp.broadcast_to(scale, (TOK, HD))
    inner = jnp.broadcast_to(inner, (TOK, HD))

    def gstates(half, g):
        def body(head, j, carry):
            at = lanes(head)
            normed = m["attn"][:, at] * scale
            grad = (scale * (m["dnorm"][:, at] - normed * inner)).astype(BF16)
            m["grad"][:, at] = grad
            term = (dy[:, at].astype(F32) * normed).reshape(TOK // 8, 8, HD).sum(axis=0)
            nth = FIRST[g] + j
            m["gain_own"][half, nth // SIDE, pl.ds(pl.multiple_of(nth % SIDE * 8, 8), 8)] = term
            m[f"own1{g}"][half, :, j] = sliced(dot(m["qt"][head], grad, 1, 0))
            return carry

        each_head(half * HALF + FIRST[g], GROUPS[g], body)

    pairs = []
    for g in range(G):
        gstates(other, g)
        pairs.append(pair_send(1, g))
    gain_step(0)

    def grads_part(head, j, carry):
        at = lanes(head)
        g_h = m["grad"][:, at]
        dmask = jnp.where(causal, dot(g_h, v[:, at], 1, 1), 0.0).astype(BF16)
        gq_ref[:, at] = (dot(dmask, k[:, at], 1, 0) + dot(g_h, m["prefix"][head], 1, 1)).astype(BF16)
        m["gk_part"][:, at] = dot(dmask, q[:, at], 0, 0)
        return carry

    def value_part(head, j, carry):
        at = lanes(head)
        m["gv_part"][:, at] = dot(m["masked"][head], m["grad"][:, at], 0, 0)
        return carry

    gain_steps = iter(range(1, 6))

    def gain_at(point):
        for _ in range(GAIN_POINTS.count(point)):
            gain_step(next(gain_steps))

    def fill(g):
        if g == 0:
            for later in range(LEAD, G):
                gstates(core, later)
        gain_at(f"F{g}")
        if g == 0:
            part(grads_part, 0)
            part(grads_part, 1)
        elif g < G - 1:
            part(grads_part, g + 1)
        else:
            each_head(0, HEADS, value_part)

    backs = exchange(1, pairs, lambda g: gstates(core, g), fill)

    gain_at("E")

    def finish(half, g, mine):
        def body(head, j, carry):
            at = lanes(head)
            s = carried(1, g, j, mine)
            gk_ref[:, at] = (m["gk_part"][:, at] + dot(v[:, at], s, 1, 1)).astype(BF16)
            gv_ref[:, at] = (m["gv_part"][:, at] + dot(k[:, at], s, 1, 0)).astype(BF16)
            return carry

        each_head(half * HALF + FIRST[g], GROUPS[g], body)

    for g in range(G):
        backs[g]()
        hand = hand_send(1, g)
        gain_at(f"B{g}")
        finish(core, g, True)
        hand()
        finish(other, g, False)
    gg_ref[pl.ds(pl.multiple_of(core * HALF, HALF), HALF)] = gain_result(m["gain_back"])
    gain_wait[5]()
    gg_ref[pl.ds(pl.multiple_of(other * HALF, HALF), HALF)] = gain_result(m["gain_taken"])
    for wait in pending:
        wait()


def write_out(*refs):
    ins, outs, sem = refs[:4], refs[4:8], refs[8]
    copies = [pltpu.make_async_copy(i, o, sem.at[n]) for n, (i, o) in enumerate(zip(ins, outs))]
    for copy in copies:
        copy.start()
    for copy in copies:
        copy.wait()


def shards(query, key_in, value_in, cotangent, gain):
    shapes = scratch_shapes()
    vmem = pl.BlockSpec(memory_space=pltpu.VMEM)
    hbm = pl.BlockSpec(memory_space=pl.ANY)
    kept = (pltpu.VMEM((TOK, F), BF16),) * 3 + (pltpu.VMEM((HEADS, HD), F32),)
    results = pl.pallas_call(
        kernel,
        out_shape=kept,
        in_specs=[hbm] * 5,
        out_specs=(vmem,) * 4,
        scratch_shapes=[shapes[n] for n in NAMES],
        compiler_params=pltpu.CompilerParams(
            collective_id=0, has_side_effects=True, vmem_limit_bytes=60 * 2**20
        ),
        name="scan_grads",
    )(query[0], key_in[0], value_in[0], cotangent[0], gain.reshape(1, F))
    gq, gk, gv, gg = pl.pallas_call(
        write_out,
        out_shape=tuple(jax.ShapeDtypeStruct(r.shape, r.dtype) for r in results),
        in_specs=[vmem] * 4,
        out_specs=(hbm,) * 4,
        scratch_shapes=[pltpu.SemaphoreType.DMA((4,))],
        compiler_params=pltpu.CompilerParams(vmem_limit_bytes=8 * 2**20),
        name="write_out",
    )(*results)
    return gq[None], gk[None], gv[None], gg.reshape(F)


def solution(mesh):
    placed = P("dp", "seq", None)
    return jax.shard_map(
        shards,
        mesh=mesh,
        in_specs=(placed, placed, placed, placed, P()),
        out_specs=(placed, placed, placed, P()),
        check_vma=False,
    )
```

```python
import functools
import math

import jax
import jax.numpy as jnp
from jax import lax
from jax.experimental import pallas as pl
from jax.experimental.pallas import tpu as pltpu
from jax.sharding import PartitionSpec as P

HD = 128
TOK = 128
HEADS = 32
F = HEADS * HD
HALF = HEADS // 2
SIDE = 4
ROWS = HD // SIDE
DP = 8
GROUPS = (2, 4, 4, 4, 2)
G = len(GROUPS)
FIRST = [sum(GROUPS[:g]) for g in range(G)]
LEAD = 2
GAIN_POINTS = ("F0", "F3", "F4", "E", "B3")
MESH = pl.DeviceIdType.MESH
F32 = jnp.float32
BF16 = jnp.bfloat16

def dot(a, b, ca, cb):
    return lax.dot_general(a, b, (((ca,), (cb,)), ((), ())), preferred_element_type=F32)


def scratch_shapes():
    shapes = {}
    for name in ("q", "k", "v", "dy"):
        shapes[name] = pltpu.VMEM((TOK, F), BF16)
    shapes["gain"] = pltpu.VMEM((1, F), F32)
    shapes["load_sem"] = pltpu.SemaphoreType.DMA((5,))
    for s in range(2):
        for g in range(G):
            n = GROUPS[g]
            shapes[f"own{s}{g}"] = pltpu.VMEM((2, SIDE, n, ROWS, HD), F32)
            shapes[f"total{s}{g}"] = pltpu.VMEM((n, ROWS, HD), F32)
            for name in ("pair", "sums", "gath", "rows", "give", "back", "hand", "taken"):
                shapes[f"{name}{s}{g}"] = pltpu.VMEM((SIDE, n, ROWS, HD), F32)
        for name in ("pair", "out", "back", "hand"):
            shapes[f"{name}_s{s}"] = pltpu.SemaphoreType.DMA((G,))
            shapes[f"{name}_r{s}"] = pltpu.SemaphoreType.DMA((G,))
        shapes[f"rows_s{s}"] = pltpu.SemaphoreType.DMA((G, SIDE - 1))
        shapes[f"rows_r{s}"] = pltpu.SemaphoreType.DMA((G, SIDE - 1))
    shapes["prefix"] = pltpu.VMEM((HEADS, HD, HD), BF16)
    shapes["masked"] = pltpu.VMEM((HEADS, TOK, TOK), BF16)
    shapes["qt"] = pltpu.VMEM((HEADS, HD, TOK), BF16)
    shapes["attn"] = pltpu.VMEM((TOK, F), F32)
    shapes["dnorm"] = pltpu.VMEM((TOK, F), F32)
    shapes["grad"] = pltpu.VMEM((TOK, F), BF16)
    shapes["gk_part"] = pltpu.VMEM((TOK, F), F32)
    shapes["gv_part"] = pltpu.VMEM((TOK, F), F32)
    shapes["gain_own"] = pltpu.VMEM((2, SIDE, ROWS, HD), F32)
    for name in ("gain_pair", "gain_sums", "gain_x", "gain_y", "gain_back", "gain_taken"):
        shapes[name] = pltpu.VMEM((SIDE, ROWS, HD), F32)
    shapes["gain_z"] = pltpu.VMEM((DP, ROWS, HD), F32)
    for name in ("gain_ysend", "gain_zsend", "gain_bsend"):
        shapes[name] = pltpu.VMEM((ROWS, HD), F32)
    shapes["gain_s"] = pltpu.SemaphoreType.DMA((6,))
    shapes["gain_r"] = pltpu.SemaphoreType.DMA((6,))
    return shapes


NAMES = list(scratch_shapes())


def kernel(q_hbm, k_hbm, v_hbm, dy_hbm, gain_hbm, gq_ref, gk_ref, gv_ref, gg_ref, *scratch):
    m = dict(zip(NAMES, scratch))
    q, k, v, dy, gain = (m[n] for n in ("q", "k", "v", "dy", "gain"))
    loads = [
        pltpu.make_async_copy(src, dst, m["load_sem"].at[i])
        for i, (src, dst) in enumerate(((k_hbm, k), (v_hbm, v), (q_hbm, q), (dy_hbm, dy), (gain_hbm, gain)))
    ]

    z = lax.axis_index("dp")
    s_at = lax.axis_index("seq")
    chip = s_at // 2
    core = s_at % 2
    other = 1 - core
    y, x = chip // SIDE, chip % SIDE

    def device(y_at, x_at, core_at):
        return (z, (y_at * SIDE + x_at) * 2 + core_at)

    partner = device(y, x, other)
    turns = [2, 1 + 2 * core, 3 - 2 * core]
    x_near = [(x + d) % SIDE for d in turns]
    x_targets = [device(y, c, core) for c in x_near]
    y_targets = [device((y + d) % SIDE, x, core) for d in turns]
    z_targets = [((z + d) % DP, s_at) for d in (1, 7, 2, 6, 3, 5, 4)]

    barrier = pltpu.get_barrier_semaphore()
    greeted = [partner] + x_targets + y_targets + z_targets
    for t in greeted:
        pl.semaphore_signal(barrier, inc=1, device_id=t, device_id_type=MESH)
    for load in loads:
        load.start()

    pending = []

    def wait_bytes(ref, sem):
        pltpu.make_async_copy(ref, ref, sem).wait()

    def remote(src, dst, ssem, rsem, target):
        copy = pltpu.make_async_remote_copy(
            src_ref=src, dst_ref=dst, send_sem=ssem, recv_sem=rsem, device_id=target, device_id_type=MESH
        )
        copy.start()
        return copy

    def fan(src_of, dst, ssem, rsem, to, whole):
        for i, target in enumerate(to):
            remote(src_of(i), dst, ssem, rsem, target)
        pending.append(lambda: wait_bytes(whole, ssem))
        return lambda: wait_bytes(whole, rsem)

    def to_partner(src, dst, ssem, rsem):
        copy = remote(src, dst, ssem, rsem, partner)
        pending.append(copy.wait_send)
        return copy.wait_recv

    def lanes(head):
        return pl.ds(pl.multiple_of(head * HD, HD), HD)

    def each_head(first, count, body, carry=0):
        step = 4 if count % 4 == 0 else 2

        def some(i, carry):
            for u in range(step):
                carry = body(first + i * step + u, i * step + u, carry)
            return carry

        return lax.fori_loop(0, count // step, some, carry)

    def sliced(value):
        return value.reshape(SIDE, ROWS, HD)

    def sems(name, scan, g):
        return m[f"{name}_s{scan}"].at[g], m[f"{name}_r{scan}"].at[g]

    def pair_send(scan, g):
        return to_partner(m[f"own{scan}{g}"].at[other], m[f"pair{scan}{g}"], *sems("pair", scan, g))

    def out_send(scan, g):
        sums, gath = m[f"sums{scan}{g}"], m[f"gath{scan}{g}"]

        def add(c, carry):
            sums[c] = m[f"own{scan}{g}"][core, c] + m[f"pair{scan}{g}"][c]
            return carry

        lax.fori_loop(0, SIDE, add, 0)
        gath[x] = sums[x]
        return fan(
            lambda i: sums.at[x_near[i]], gath.at[x], *sems("out", scan, g), x_targets, gath.at[pl.ds(0, SIDE - 1)]
        )

    def rows_send(scan, g):
        gath, total, rows = m[f"gath{scan}{g}"], m[f"total{scan}{g}"], m[f"rows{scan}{g}"]

        def one(j, carry):
            value = (gath[0, j] + gath[1, j]) + (gath[2, j] + gath[3, j])
            total[j] = value
            rows[y, j] = value
            return carry

        lax.fori_loop(0, GROUPS[g], one, 0)
        sign = 1 if scan == 0 else -1

        def in_side(at):
            return (at >= 0) & (at < SIDE)

        def copy(d):
            return pltpu.make_async_remote_copy(
                src_ref=total,
                dst_ref=rows.at[y],
                send_sem=m[f"rows_s{scan}"].at[g, d - 1],
                recv_sem=m[f"rows_r{scan}"].at[g, d - 1],
                device_id=device((y + sign * d + SIDE) % SIDE, x, core),
                device_id_type=MESH,
            )

        def each(active, act):
            for d in range(1, SIDE):
                pl.when(active(d))(lambda d=d: act(d))

        each(lambda d: in_side(y + sign * d), lambda d: copy(d).start())
        pending.append(lambda: each(lambda d: in_side(y + sign * d), lambda d: copy(d).wait_send()))
        return lambda: each(lambda d: in_side(y - sign * d), lambda d: copy(d).wait_recv())

    def back_send(scan, g):
        gath, rows, give, back = (m[f"{name}{scan}{g}"] for name in ("gath", "rows", "give", "back"))

        def one(j, carry):
            value = jnp.zeros((ROWS, HD), F32)
            for c in range(SIDE):
                value = value + jnp.where(c < y if scan == 0 else c > y, rows[c, j], 0.0)
            for c in range(SIDE) if scan == 0 else reversed(range(SIDE)):
                give[c, j] = value
                value = value + gath[c, j]
            return carry

        lax.fori_loop(0, GROUPS[g], one, 0)
        back[x] = give[x]
        return fan(
            lambda i: give.at[x_near[i]],
            back.at[x],
            *sems("back", scan, g),
            x_targets,
            back.at[pl.ds(0, SIDE - 1)],
        )

    def hand_send(scan, g):
        hand, back, own = (m[f"{name}{scan}{g}"] for name in ("hand", "back", "own"))
        with_own = jnp.where(core == (0 if scan == 0 else 1), 1.0, 0.0).astype(F32)

        def add(c, carry):
            hand[c] = back[c] + own[core, c] * with_own
            return carry

        lax.fori_loop(0, SIDE, add, 0)
        return to_partner(hand, m[f"taken{scan}{g}"], *sems("hand", scan, g))

    def carried(scan, g, j, mine):
        if mine:
            with_pair = jnp.where(core == (1 if scan == 0 else 0), 1.0, 0.0).astype(F32)
            value = m[f"back{scan}{g}"][:, j] + m[f"pair{scan}{g}"][:, j] * with_pair
        else:
            value = m[f"taken{scan}{g}"][:, j]
        return value.reshape(HD, HD).astype(BF16)

    def exchange(scan, make, fill):
        pairs, outs, totals, backs = [], [], [], []

        def pair(g):
            make(other, g)
            pairs.append(pair_send(scan, g))

        for g in range(LEAD):
            pair(g)
        for g in range(LEAD):
            make(core, g)
            pairs[g]()
            outs.append(out_send(scan, g))
            if LEAD + g < G:
                pair(LEAD + g)
        for g in range(2 * LEAD, G):
            pair(g)
        for g in range(G):
            fill(g)
            outs[g]()
            totals.append(rows_send(scan, g))
            if g + LEAD < G:
                pairs[g + LEAD]()
                outs.append(out_send(scan, g + LEAD))
            if g >= 1:
                totals[g - 1]()
                backs.append(back_send(scan, g - 1))
        totals[G - 1]()
        backs.append(back_send(scan, G - 1))
        return backs

    def drain():
        for wait in pending:
            wait()
        pending.clear()

    gain_wait = []

    def gain_step(at):
        step_sems = (m["gain_s"].at[at], m["gain_r"].at[at])
        if at:
            gain_wait[at - 1]()
        if at == 0:
            wait = to_partner(m["gain_own"].at[other], m["gain_pair"], *step_sems)
        elif at == 1:
            sums, got = m["gain_sums"], m["gain_x"]
            sums[...] = m["gain_own"][core] + m["gain_pair"][...]
            got[x] = sums[x]
            wait = fan(lambda i: sums.at[x_near[i]], got.at[x], *step_sems, x_targets, got.at[pl.ds(0, SIDE - 1)])
        elif at == 2:
            wait = gain_fan("gain_x", "gain_ysend", "gain_y", y, y_targets, step_sems)
        elif at == 3:
            wait = gain_fan("gain_y", "gain_zsend", "gain_z", z, z_targets, step_sems)
        elif at == 4:
            wait = gain_fan("gain_z", "gain_bsend", "gain_back", x, x_targets, step_sems)
        else:
            wait = to_partner(m["gain_back"], m["gain_taken"], *step_sems)
        gain_wait.append(wait)

    def gain_fan(src, send, dst, slot, to, step_sems):
        value = jnp.sum(m[src][...], axis=0)
        m[send][...] = value
        m[dst][slot] = value
        return fan(lambda i: m[send], m[dst].at[slot], *step_sems, to, m[dst].at[pl.ds(0, len(to))])

    def gain_result(ref):
        total = ref[...].reshape(HALF, 8, HD).sum(axis=1)
        return total * (1.0 / math.sqrt(DP * 32 * TOK))

    def states(half, g):
        def body(head, j, carry):
            at = lanes(head)
            m[f"own0{g}"][half, :, j] = sliced(dot(k[:, at], v[:, at], 0, 0))
            return carry

        each_head(half * HALF + FIRST[g], GROUPS[g], body)

    loads[0].wait()
    loads[1].wait()
    for g in range(G):
        states(other, g)
        states(core, g)
    pl.semaphore_wait(barrier, len(greeted))

    rows = lax.broadcasted_iota(jnp.int32, (TOK, TOK), 0)
    cols = lax.broadcasted_iota(jnp.int32, (TOK, TOK), 1)
    causal = rows >= cols

    def local_part(head, j, carry):
        at = lanes(head)
        scores = jnp.where(causal, dot(q[:, at], k[:, at], 1, 1), 0.0).astype(BF16)
        m["masked"][head] = scores
        m["attn"][:, at] = dot(scores, v[:, at], 1, 0)
        return carry

    def later_part(head, j, carry):
        at = lanes(head)
        m["dnorm"][:, at] = dy[:, at].astype(F32) * gain[:, at]
        m["qt"][head] = q[:, at].T
        return carry

    def part(body, g):
        each_head(2 * FIRST[g], 2 * GROUPS[g], body)

    def fill(g):
        if g == 0:
            for load in loads[2:]:
                load.wait()
            part(local_part, 0)
            part(local_part, 1)
        elif g < G - 1:
            part(local_part, g + 1)
        else:
            each_head(0, HEADS, later_part)

    backs = exchange(0, lambda half, g: None, fill)

    def attn_part(half, g, mine, acc):
        def body(head, j, acc):
            sq, cross = acc
            at = lanes(head)
            p = carried(0, g, j, mine)
            m["prefix"][head] = p
            a = m["attn"][:, at] + dot(q[:, at], p, 1, 0)
            m["attn"][:, at] = a
            return (sq + a * a, cross + a * m["dnorm"][:, at])

        return each_head(half * HALF + FIRST[g], GROUPS[g], body, acc)

    acc = (jnp.zeros((TOK, HD), F32), jnp.zeros((TOK, HD), F32))
    hands = []
    for g in range(G):
        backs[g]()
        hands.append(hand_send(0, g))
        acc = attn_part(core, g, True, acc)
    for g in range(G):
        hands[g]()
        acc = attn_part(other, g, False, acc)
    sq, cross = acc
    scale = lax.rsqrt(jnp.sum(sq, axis=1, keepdims=True) * (1.0 / F) + 1e-06)
    inner = scale * (jnp.sum(cross, axis=1, keepdims=True) * (1.0 / F))
    scale = jnp.broadcast_to(scale, (TOK, HD))
    inner = jnp.broadcast_to(inner, (TOK, HD))

    def gstates(half, g):
        def body(head, j, carry):
            at = lanes(head)
            normed = m["attn"][:, at] * scale
            grad = (scale * (m["dnorm"][:, at] - normed * inner)).astype(BF16)
            m["grad"][:, at] = grad
            term = (dy[:, at].astype(F32) * normed).reshape(TOK // 8, 8, HD).sum(axis=0)
            nth = FIRST[g] + j
            m["gain_own"][half, nth // SIDE, pl.ds(pl.multiple_of(nth % SIDE * 8, 8), 8)] = term
            m[f"own1{g}"][half, :, j] = sliced(dot(m["qt"][head], grad, 1, 0))
            return carry

        each_head(half * HALF + FIRST[g], GROUPS[g], body)

    def grads_part(head, j, carry):
        at = lanes(head)
        g_h = m["grad"][:, at]
        dmask = jnp.where(causal, dot(g_h, v[:, at], 1, 1), 0.0).astype(BF16)
        gq_ref[:, at] = (dot(dmask, k[:, at], 1, 0) + dot(g_h, m["prefix"][head], 1, 1)).astype(BF16)
        m["gk_part"][:, at] = dot(dmask, q[:, at], 0, 0)
        return carry

    def value_part(head, j, carry):
        at = lanes(head)
        m["gv_part"][:, at] = dot(m["masked"][head], m["grad"][:, at], 0, 0)
        return carry

    gain_steps = iter(range(1, 6))

    def gain_at(point):
        for _ in range(GAIN_POINTS.count(point)):
            gain_step(next(gain_steps))

    def fill(g):
        if g == 0:
            gain_step(0)
            for later in range(LEAD, G):
                gstates(core, later)
        gain_at(f"F{g}")
        if g == 0:
            part(grads_part, 0)
            part(grads_part, 1)
        elif g < G - 1:
            part(grads_part, g + 1)
        else:
            each_head(0, HEADS, value_part)

    backs = exchange(1, gstates, fill)

    gain_at("E")

    def finish(half, g, mine):
        def body(head, j, carry):
            at = lanes(head)
            s = carried(1, g, j, mine)
            gk_ref[:, at] = (m["gk_part"][:, at] + dot(v[:, at], s, 1, 1)).astype(BF16)
            gv_ref[:, at] = (m["gv_part"][:, at] + dot(k[:, at], s, 1, 0)).astype(BF16)
            return carry

        each_head(half * HALF + FIRST[g], GROUPS[g], body)

    drain()
    hands = []
    for g in range(G):
        backs[g]()
        hands.append(hand_send(1, g))
        gain_at(f"B{g}")
        finish(core, g, True)
    for g in range(G):
        hands[g]()
        finish(other, g, False)
    gg_ref[pl.ds(pl.multiple_of(core * HALF, HALF), HALF)] = gain_result(m["gain_back"])
    gain_wait[5]()
    gg_ref[pl.ds(pl.multiple_of(other * HALF, HALF), HALF)] = gain_result(m["gain_taken"])
    drain()


def write_out(*refs):
    ins, outs, sem = refs[:4], refs[4:8], refs[8]
    copies = [pltpu.make_async_copy(i, o, sem.at[n]) for n, (i, o) in enumerate(zip(ins, outs))]
    for copy in copies:
        copy.start()
    for copy in copies:
        copy.wait()


def shards(query, key_in, value_in, cotangent, gain):
    shapes = scratch_shapes()
    vmem = pl.BlockSpec(memory_space=pltpu.VMEM)
    hbm = pl.BlockSpec(memory_space=pl.ANY)
    kept = (pltpu.VMEM((TOK, F), BF16),) * 3 + (pltpu.VMEM((HEADS, HD), F32),)
    results = pl.pallas_call(
        kernel,
        out_shape=kept,
        in_specs=[hbm] * 5,
        out_specs=(vmem,) * 4,
        scratch_shapes=[shapes[n] for n in NAMES],
        compiler_params=pltpu.CompilerParams(
            collective_id=0, has_side_effects=True, vmem_limit_bytes=60 * 2**20
        ),
        name="scan_grads",
    )(query[0], key_in[0], value_in[0], cotangent[0], gain.reshape(1, F))
    gq, gk, gv, gg = pl.pallas_call(
        write_out,
        out_shape=tuple(jax.ShapeDtypeStruct(r.shape, r.dtype) for r in results),
        in_specs=[vmem] * 4,
        out_specs=(hbm,) * 4,
        scratch_shapes=[pltpu.SemaphoreType.DMA((4,))],
        compiler_params=pltpu.CompilerParams(vmem_limit_bytes=8 * 2**20),
        name="write_out",
    )(*results)
    return gq[None], gk[None], gv[None], gg.reshape(F)


def solution(mesh):
    placed = P("dp", "seq", None)
    return jax.shard_map(
        shards,
        mesh=mesh,
        in_specs=(placed, placed, placed, placed, P()),
        out_specs=(placed, placed, placed, P()),
        check_vma=False,
    )
```

```python
import functools
import math

import jax
import jax.numpy as jnp
from jax import lax
from jax.experimental import pallas as pl
from jax.experimental.pallas import tpu as pltpu
from jax.sharding import PartitionSpec as P

HD = 128
TOK = 128
HEADS = 32
F = HEADS * HD
HALF = HEADS // 2
SIDE = 4
ROWS = HD // SIDE
DP = 8
GROUPS = (2, 2, 4, 4, 2, 2)
G = len(GROUPS)
FIRST = [sum(GROUPS[:g]) for g in range(G)]
LEAD = 3
GAIN_POINTS = ("F0", "F3", "F5", "E", "B4")
MESH = pl.DeviceIdType.MESH
F32 = jnp.float32
BF16 = jnp.bfloat16

def dot(a, b, ca, cb):
    return lax.dot_general(a, b, (((ca,), (cb,)), ((), ())), preferred_element_type=F32)


def scratch_shapes():
    shapes = {}
    for name in ("q", "k", "v", "dy"):
        shapes[name] = pltpu.VMEM((TOK, F), BF16)
    shapes["gain"] = pltpu.VMEM((1, F), F32)
    shapes["load_sem"] = pltpu.SemaphoreType.DMA((5,))
    for s in range(2):
        for g in range(G):
            n = GROUPS[g]
            shapes[f"own{s}{g}"] = pltpu.VMEM((2, SIDE, n, ROWS, HD), F32)
            shapes[f"total{s}{g}"] = pltpu.VMEM((n, ROWS, HD), F32)
            for name in ("pair", "sums", "gath", "rows", "give", "back", "hand", "taken"):
                shapes[f"{name}{s}{g}"] = pltpu.VMEM((SIDE, n, ROWS, HD), F32)
        for name in ("pair", "out", "back", "hand"):
            shapes[f"{name}_s{s}"] = pltpu.SemaphoreType.DMA((G,))
            shapes[f"{name}_r{s}"] = pltpu.SemaphoreType.DMA((G,))
        shapes[f"rows_s{s}"] = pltpu.SemaphoreType.DMA((G, SIDE - 1))
        shapes[f"rows_r{s}"] = pltpu.SemaphoreType.DMA((G, SIDE - 1))
    shapes["prefix"] = pltpu.VMEM((HEADS, HD, HD), BF16)
    shapes["masked"] = pltpu.VMEM((HEADS, TOK, TOK), BF16)
    shapes["qt"] = pltpu.VMEM((HEADS, HD, TOK), BF16)
    shapes["attn"] = pltpu.VMEM((TOK, F), F32)
    shapes["dnorm"] = pltpu.VMEM((TOK, F), F32)
    shapes["grad"] = pltpu.VMEM((TOK, F), BF16)
    shapes["gk_part"] = pltpu.VMEM((TOK, F), F32)
    shapes["gv_part"] = pltpu.VMEM((TOK, F), F32)
    shapes["gain_own"] = pltpu.VMEM((2, SIDE, ROWS, HD), F32)
    for name in ("gain_pair", "gain_sums", "gain_x", "gain_y", "gain_back", "gain_taken"):
        shapes[name] = pltpu.VMEM((SIDE, ROWS, HD), F32)
    shapes["gain_z"] = pltpu.VMEM((DP, ROWS, HD), F32)
    for name in ("gain_ysend", "gain_zsend", "gain_bsend"):
        shapes[name] = pltpu.VMEM((ROWS, HD), F32)
    shapes["gain_s"] = pltpu.SemaphoreType.DMA((6,))
    shapes["gain_r"] = pltpu.SemaphoreType.DMA((6,))
    return shapes


NAMES = list(scratch_shapes())


def kernel(q_hbm, k_hbm, v_hbm, dy_hbm, gain_hbm, gq_ref, gk_ref, gv_ref, gg_ref, *scratch):
    m = dict(zip(NAMES, scratch))
    q, k, v, dy, gain = (m[n] for n in ("q", "k", "v", "dy", "gain"))
    loads = [
        pltpu.make_async_copy(src, dst, m["load_sem"].at[i])
        for i, (src, dst) in enumerate(((k_hbm, k), (v_hbm, v), (q_hbm, q), (dy_hbm, dy), (gain_hbm, gain)))
    ]

    z = lax.axis_index("dp")
    s_at = lax.axis_index("seq")
    chip = s_at // 2
    core = s_at % 2
    other = 1 - core
    y, x = chip // SIDE, chip % SIDE

    def device(y_at, x_at, core_at):
        return (z, (y_at * SIDE + x_at) * 2 + core_at)

    partner = device(y, x, other)
    turns = [2, 1 + 2 * core, 3 - 2 * core]
    x_near = [(x + d) % SIDE for d in turns]
    x_targets = [device(y, c, core) for c in x_near]
    y_targets = [device((y + d) % SIDE, x, core) for d in turns]
    z_targets = [((z + d) % DP, s_at) for d in (1, 7, 2, 6, 3, 5, 4)]

    barrier = pltpu.get_barrier_semaphore()
    greeted = [partner] + x_targets + y_targets + z_targets
    for t in greeted:
        pl.semaphore_signal(barrier, inc=1, device_id=t, device_id_type=MESH)
    for load in loads:
        load.start()

    pending = []

    def wait_bytes(ref, sem):
        pltpu.make_async_copy(ref, ref, sem).wait()

    def remote(src, dst, ssem, rsem, target):
        copy = pltpu.make_async_remote_copy(
            src_ref=src, dst_ref=dst, send_sem=ssem, recv_sem=rsem, device_id=target, device_id_type=MESH
        )
        copy.start()
        return copy

    def fan(src_of, dst, ssem, rsem, to, whole):
        for i, target in enumerate(to):
            remote(src_of(i), dst, ssem, rsem, target)
        pending.append(lambda: wait_bytes(whole, ssem))
        return lambda: wait_bytes(whole, rsem)

    def to_partner(src, dst, ssem, rsem):
        copy = remote(src, dst, ssem, rsem, partner)
        pending.append(copy.wait_send)
        return copy.wait_recv

    def lanes(head):
        return pl.ds(pl.multiple_of(head * HD, HD), HD)

    def each_head(first, count, body, carry=0):
        step = 4 if count % 4 == 0 else 2

        def some(i, carry):
            for u in range(step):
                carry = body(first + i * step + u, i * step + u, carry)
            return carry

        return lax.fori_loop(0, count // step, some, carry)

    def sliced(value):
        return value.reshape(SIDE, ROWS, HD)

    def sems(name, scan, g):
        return m[f"{name}_s{scan}"].at[g], m[f"{name}_r{scan}"].at[g]

    def pair_send(scan, g):
        return to_partner(m[f"own{scan}{g}"].at[other], m[f"pair{scan}{g}"], *sems("pair", scan, g))

    def out_send(scan, g):
        sums, gath = m[f"sums{scan}{g}"], m[f"gath{scan}{g}"]

        def add(c, carry):
            sums[c] = m[f"own{scan}{g}"][core, c] + m[f"pair{scan}{g}"][c]
            return carry

        lax.fori_loop(0, SIDE, add, 0)
        gath[x] = sums[x]
        return fan(
            lambda i: sums.at[x_near[i]], gath.at[x], *sems("out", scan, g), x_targets, gath.at[pl.ds(0, SIDE - 1)]
        )

    def rows_send(scan, g):
        gath, total, rows = m[f"gath{scan}{g}"], m[f"total{scan}{g}"], m[f"rows{scan}{g}"]

        def one(j, carry):
            value = (gath[0, j] + gath[1, j]) + (gath[2, j] + gath[3, j])
            total[j] = value
            rows[y, j] = value
            return carry

        lax.fori_loop(0, GROUPS[g], one, 0)
        sign = 1 if scan == 0 else -1

        def in_side(at):
            return (at >= 0) & (at < SIDE)

        def copy(d):
            return pltpu.make_async_remote_copy(
                src_ref=total,
                dst_ref=rows.at[y],
                send_sem=m[f"rows_s{scan}"].at[g, d - 1],
                recv_sem=m[f"rows_r{scan}"].at[g, d - 1],
                device_id=device((y + sign * d + SIDE) % SIDE, x, core),
                device_id_type=MESH,
            )

        def each(active, act):
            for d in range(1, SIDE):
                pl.when(active(d))(lambda d=d: act(d))

        each(lambda d: in_side(y + sign * d), lambda d: copy(d).start())
        pending.append(lambda: each(lambda d: in_side(y + sign * d), lambda d: copy(d).wait_send()))
        return lambda: each(lambda d: in_side(y - sign * d), lambda d: copy(d).wait_recv())

    def back_send(scan, g):
        gath, rows, give, back = (m[f"{name}{scan}{g}"] for name in ("gath", "rows", "give", "back"))

        def one(j, carry):
            value = jnp.zeros((ROWS, HD), F32)
            for c in range(SIDE):
                value = value + jnp.where(c < y if scan == 0 else c > y, rows[c, j], 0.0)
            for c in range(SIDE) if scan == 0 else reversed(range(SIDE)):
                give[c, j] = value
                value = value + gath[c, j]
            return carry

        lax.fori_loop(0, GROUPS[g], one, 0)
        back[x] = give[x]
        return fan(
            lambda i: give.at[x_near[i]],
            back.at[x],
            *sems("back", scan, g),
            x_targets,
            back.at[pl.ds(0, SIDE - 1)],
        )

    def hand_send(scan, g):
        hand, back, own = (m[f"{name}{scan}{g}"] for name in ("hand", "back", "own"))
        with_own = jnp.where(core == (0 if scan == 0 else 1), 1.0, 0.0).astype(F32)

        def add(c, carry):
            hand[c] = back[c] + own[core, c] * with_own
            return carry

        lax.fori_loop(0, SIDE, add, 0)
        return to_partner(hand, m[f"taken{scan}{g}"], *sems("hand", scan, g))

    def carried(scan, g, j, mine):
        if mine:
            with_pair = jnp.where(core == (1 if scan == 0 else 0), 1.0, 0.0).astype(F32)
            value = m[f"back{scan}{g}"][:, j] + m[f"pair{scan}{g}"][:, j] * with_pair
        else:
            value = m[f"taken{scan}{g}"][:, j]
        return value.reshape(HD, HD).astype(BF16)

    def exchange(scan, make, fill):
        pairs, outs, totals, backs = [], [], [], []

        def pair(g):
            make(other, g)
            pairs.append(pair_send(scan, g))

        for g in range(LEAD):
            pair(g)
        for g in range(LEAD):
            make(core, g)
            pairs[g]()
            outs.append(out_send(scan, g))
            if LEAD + g < G:
                pair(LEAD + g)
        for g in range(2 * LEAD, G):
            pair(g)
        for g in range(G):
            fill(g)
            outs[g]()
            totals.append(rows_send(scan, g))
            if g + LEAD < G:
                pairs[g + LEAD]()
                outs.append(out_send(scan, g + LEAD))
            if g >= 1:
                totals[g - 1]()
                backs.append(back_send(scan, g - 1))
        totals[G - 1]()
        backs.append(back_send(scan, G - 1))
        return backs

    def drain():
        for wait in pending:
            wait()
        pending.clear()

    gain_wait = []

    def gain_step(at):
        step_sems = (m["gain_s"].at[at], m["gain_r"].at[at])
        if at:
            gain_wait[at - 1]()
        if at == 0:
            wait = to_partner(m["gain_own"].at[other], m["gain_pair"], *step_sems)
        elif at == 1:
            sums, got = m["gain_sums"], m["gain_x"]
            sums[...] = m["gain_own"][core] + m["gain_pair"][...]
            got[x] = sums[x]
            wait = fan(lambda i: sums.at[x_near[i]], got.at[x], *step_sems, x_targets, got.at[pl.ds(0, SIDE - 1)])
        elif at == 2:
            wait = gain_fan("gain_x", "gain_ysend", "gain_y", y, y_targets, step_sems)
        elif at == 3:
            wait = gain_fan("gain_y", "gain_zsend", "gain_z", z, z_targets, step_sems)
        elif at == 4:
            wait = gain_fan("gain_z", "gain_bsend", "gain_back", x, x_targets, step_sems)
        else:
            wait = to_partner(m["gain_back"], m["gain_taken"], *step_sems)
        gain_wait.append(wait)

    def gain_fan(src, send, dst, slot, to, step_sems):
        value = jnp.sum(m[src][...], axis=0)
        m[send][...] = value
        m[dst][slot] = value
        return fan(lambda i: m[send], m[dst].at[slot], *step_sems, to, m[dst].at[pl.ds(0, len(to))])

    def gain_result(ref):
        total = ref[...].reshape(HALF, 8, HD).sum(axis=1)
        return total * (1.0 / math.sqrt(DP * 32 * TOK))

    def states(half, g):
        def body(head, j, carry):
            at = lanes(head)
            m[f"own0{g}"][half, :, j] = sliced(dot(k[:, at], v[:, at], 0, 0))
            return carry

        each_head(half * HALF + FIRST[g], GROUPS[g], body)

    loads[0].wait()
    loads[1].wait()
    for g in range(G):
        states(other, g)
        states(core, g)
    pl.semaphore_wait(barrier, len(greeted))

    rows = lax.broadcasted_iota(jnp.int32, (TOK, TOK), 0)
    cols = lax.broadcasted_iota(jnp.int32, (TOK, TOK), 1)
    causal = rows >= cols

    def local_part(head, j, carry):
        at = lanes(head)
        scores = jnp.where(causal, dot(q[:, at], k[:, at], 1, 1), 0.0).astype(BF16)
        m["masked"][head] = scores
        m["attn"][:, at] = dot(scores, v[:, at], 1, 0)
        return carry

    def later_part(head, j, carry):
        at = lanes(head)
        m["dnorm"][:, at] = dy[:, at].astype(F32) * gain[:, at]
        m["qt"][head] = q[:, at].T
        return carry

    def part(body, g):
        each_head(2 * FIRST[g], 2 * GROUPS[g], body)

    def fill(g):
        if g == 0:
            for load in loads[2:]:
                load.wait()
            part(local_part, 0)
            part(local_part, 1)
        elif g < G - 1:
            part(local_part, g + 1)
        else:
            each_head(0, HEADS, later_part)

    backs = exchange(0, lambda half, g: None, fill)

    def attn_part(half, g, mine, acc):
        def body(head, j, acc):
            sq, cross = acc
            at = lanes(head)
            p = carried(0, g, j, mine)
            m["prefix"][head] = p
            a = m["attn"][:, at] + dot(q[:, at], p, 1, 0)
            m["attn"][:, at] = a
            return (sq + a * a, cross + a * m["dnorm"][:, at])

        return each_head(half * HALF + FIRST[g], GROUPS[g], body, acc)

    acc = (jnp.zeros((TOK, HD), F32), jnp.zeros((TOK, HD), F32))
    hands = []
    for g in range(G):
        backs[g]()
        hands.append(hand_send(0, g))
        acc = attn_part(core, g, True, acc)
    for g in range(G):
        hands[g]()
        acc = attn_part(other, g, False, acc)
    sq, cross = acc
    scale = lax.rsqrt(jnp.sum(sq, axis=1, keepdims=True) * (1.0 / F) + 1e-06)
    inner = scale * (jnp.sum(cross, axis=1, keepdims=True) * (1.0 / F))
    scale = jnp.broadcast_to(scale, (TOK, HD))
    inner = jnp.broadcast_to(inner, (TOK, HD))

    def gstates(half, g):
        def body(head, j, carry):
            at = lanes(head)
            normed = m["attn"][:, at] * scale
            grad = (scale * (m["dnorm"][:, at] - normed * inner)).astype(BF16)
            m["grad"][:, at] = grad
            term = (dy[:, at].astype(F32) * normed).reshape(TOK // 8, 8, HD).sum(axis=0)
            nth = FIRST[g] + j
            m["gain_own"][half, nth // SIDE, pl.ds(pl.multiple_of(nth % SIDE * 8, 8), 8)] = term
            m[f"own1{g}"][half, :, j] = sliced(dot(m["qt"][head], grad, 1, 0))
            return carry

        each_head(half * HALF + FIRST[g], GROUPS[g], body)

    def grads_part(head, j, carry):
        at = lanes(head)
        g_h = m["grad"][:, at]
        dmask = jnp.where(causal, dot(g_h, v[:, at], 1, 1), 0.0).astype(BF16)
        gq_ref[:, at] = (dot(dmask, k[:, at], 1, 0) + dot(g_h, m["prefix"][head], 1, 1)).astype(BF16)
        m["gk_part"][:, at] = dot(dmask, q[:, at], 0, 0)
        return carry

    def value_part(head, j, carry):
        at = lanes(head)
        m["gv_part"][:, at] = dot(m["masked"][head], m["grad"][:, at], 0, 0)
        return carry

    gain_steps = iter(range(1, 6))

    def gain_at(point):
        for _ in range(GAIN_POINTS.count(point)):
            gain_step(next(gain_steps))

    def fill(g):
        if g == 0:
            gain_step(0)
            for later in range(LEAD, G):
                gstates(core, later)
        gain_at(f"F{g}")
        if g == 0:
            part(grads_part, 0)
            part(grads_part, 1)
        elif g < G - 1:
            part(grads_part, g + 1)
        else:
            each_head(0, HEADS, value_part)

    backs = exchange(1, gstates, fill)

    gain_at("E")

    def finish(half, g, mine):
        def body(head, j, carry):
            at = lanes(head)
            s = carried(1, g, j, mine)
            gk_ref[:, at] = (m["gk_part"][:, at] + dot(v[:, at], s, 1, 1)).astype(BF16)
            gv_ref[:, at] = (m["gv_part"][:, at] + dot(k[:, at], s, 1, 0)).astype(BF16)
            return carry

        each_head(half * HALF + FIRST[g], GROUPS[g], body)

    drain()
    hands = []
    for g in range(G):
        backs[g]()
        hands.append(hand_send(1, g))
        gain_at(f"B{g}")
        finish(core, g, True)
    for g in range(G):
        hands[g]()
        finish(other, g, False)
    gg_ref[pl.ds(pl.multiple_of(core * HALF, HALF), HALF)] = gain_result(m["gain_back"])
    gain_wait[5]()
    gg_ref[pl.ds(pl.multiple_of(other * HALF, HALF), HALF)] = gain_result(m["gain_taken"])
    drain()


def write_out(*refs):
    ins, outs, sem = refs[:4], refs[4:8], refs[8]
    copies = [pltpu.make_async_copy(i, o, sem.at[n]) for n, (i, o) in enumerate(zip(ins, outs))]
    for copy in copies:
        copy.start()
    for copy in copies:
        copy.wait()


def shards(query, key_in, value_in, cotangent, gain):
    shapes = scratch_shapes()
    vmem = pl.BlockSpec(memory_space=pltpu.VMEM)
    hbm = pl.BlockSpec(memory_space=pl.ANY)
    kept = (pltpu.VMEM((TOK, F), BF16),) * 3 + (pltpu.VMEM((HEADS, HD), F32),)
    results = pl.pallas_call(
        kernel,
        out_shape=kept,
        in_specs=[hbm] * 5,
        out_specs=(vmem,) * 4,
        scratch_shapes=[shapes[n] for n in NAMES],
        compiler_params=pltpu.CompilerParams(
            collective_id=0, has_side_effects=True, vmem_limit_bytes=60 * 2**20
        ),
        name="scan_grads",
    )(query[0], key_in[0], value_in[0], cotangent[0], gain.reshape(1, F))
    gq, gk, gv, gg = pl.pallas_call(
        write_out,
        out_shape=tuple(jax.ShapeDtypeStruct(r.shape, r.dtype) for r in results),
        in_specs=[vmem] * 4,
        out_specs=(hbm,) * 4,
        scratch_shapes=[pltpu.SemaphoreType.DMA((4,))],
        compiler_params=pltpu.CompilerParams(vmem_limit_bytes=8 * 2**20),
        name="write_out",
    )(*results)
    return gq[None], gk[None], gv[None], gg.reshape(F)


def solution(mesh):
    placed = P("dp", "seq", None)
    return jax.shard_map(
        shards,
        mesh=mesh,
        in_specs=(placed, placed, placed, placed, P()),
        out_specs=(placed, placed, placed, P()),
        check_vma=False,
    )
```
